32 devices in a mesh: dp: 4 (over z), cell: 8 (over y, x, core).
Axes of the slice: x: 2, y: 2, z: 4, core: 2. Of those that a mesh axis runs over, the one named last changes fastest.
Arguments:
- sensitivity: float32 [1024, 65536], P(('dp', 'cell')), may hold values from -0.046875 to 0.046875
- row_period: int32 [1024], P(('dp', 'cell')), may hold values from 0 to 31
- row_site: int32 [1024], P(('dp', 'cell')), may hold values from 0 to 127
- period_err: float32 [32], replicated, may hold values from 0.2 to 2
- site_err: float32 [128], replicated, may hold values from 0.2 to 2
- cell_var: float32 [65536], replicated, may hold values from 0.25 to 4
- cell_perm: int32 [65536], replicated, may hold values from 0 to 65535, each once
Outputs:
- gram: float32 [1024, 1024], P('cell', 'dp')
The draws below stay inside these ranges and needn't reach their ends.
Inputs may be any that keep to these rules, and one draw needn't show every extreme that they name: `cell_perm`: a permutation of 0 to 65535.
All inputs are finite; a program needn't handle non-finite values.
Results may differ from the reference program's by a relative error of at most 0.0009.
Values may be sent and summed in bfloat16 or wider, within the bound.
A program may use at most 128 MiB of HBM per device.

```python
import math
import jax
import jax.numpy as jnp
from jax import lax

NCELL = 65536
NPER = 32
NSITE = 128
ND = 1024


def set_ends(drawn, rng, low, top_value):
    longest = drawn.shape.index(max(drawn.shape))
    spots = []
    for shift in (0, 1):
        where = [jax.random.randint(jax.random.fold_in(rng, axis), (), 0, length) for axis, length in enumerate(drawn.shape)]
        where[longest] = (where[longest] + shift) % drawn.shape[longest]
        spots.append(tuple(where))
    return drawn.at[spots[0]].set(low).at[spots[1]].set(top_value)


def with_spikes(entries, stream_key, source, target, blocks, factor):
    def block_of(dim):
        return (jnp.arange(entries.shape[dim]) // (entries.shape[dim] // blocks)).reshape((-1,) + (1,) * (entries.ndim - 1 - dim))

    first = jax.random.permutation(stream_key, blocks)[block_of(target)]
    second = (block_of(target) + blocks // 2) % blocks
    return jnp.where((block_of(source) == first) | (block_of(source) == second), factor * entries, entries)


def block_scale(rng, shape, split, low, top_value):
    gain, own = 1.0, jax.random.fold_in(rng, 6)
    for dim, blocks in split:
        heights = jnp.exp(jax.random.uniform(jax.random.fold_in(own, dim), (blocks,), jnp.float32, low / len(split), top_value / len(split)))
        gain = gain * jnp.repeat(heights, shape[dim] // blocks).reshape([-1 if axis == dim else 1 for axis in range(len(shape))])
    return gain


def heavy_noise(key, dims, spread, reach, cuts, heavy, kind=jnp.bfloat16):
    array = spread * jax.random.normal(key, dims, jnp.float32)
    if cuts:
        array = array * block_scale(key, dims, cuts, -0.22, 0.18)
    return jnp.clip(with_spikes(array, jax.random.fold_in(key, 3), *heavy), -reach, reach).astype(kind)


def setup_inputs(seed: int = 0) -> dict:
    streams_of = jax.random.split(jax.random.key(seed), 8)
    return {
        "sensitivity": heavy_noise(streams_of[0], (ND, NCELL), NCELL ** -0.5, 0.046875, ((0, 32),), (1, 0, 32, 2.75), jnp.float32),
        "row_period": set_ends(jax.random.randint(streams_of[1], (ND,), 0, NPER), jax.random.fold_in(streams_of[1], 1), 0, NPER - 1).astype(jnp.int32),
        "row_site": set_ends(jax.random.randint(streams_of[2], (ND,), 0, NSITE), jax.random.fold_in(streams_of[2], 1), 0, NSITE - 1).astype(jnp.int32),
        "period_err": jnp.clip(jnp.exp(jax.random.uniform(streams_of[3], (NPER,), jnp.float32, math.log(0.2), math.log(2.0))), 0.2, 2.0),
        "site_err": jnp.clip(jnp.exp(jax.random.uniform(streams_of[4], (NSITE,), jnp.float32, math.log(0.2), math.log(2.0))), 0.2, 2.0),
        "cell_var": jnp.clip(jnp.exp(jax.random.uniform(streams_of[5], (NCELL,), jnp.float32, math.log(0.25), math.log(4.0))), 0.25, 4.0),
        "cell_perm": jax.random.permutation(streams_of[6], NCELL).astype(jnp.int32),
    }


def reference(sensitivity, row_period, row_site, period_err, site_err, cell_var, cell_perm):
    period_scale = period_err[row_period]
    site_scale = site_err[row_site]
    row_weight = 1.0 / jnp.sqrt(period_scale * period_scale + site_scale * site_scale)
    scaled = (row_weight[:, None] * sensitivity).astype(jnp.bfloat16)
    column_var = cell_var[cell_perm]
    weighted = (scaled.astype(jnp.float32) * column_var[None, :]).astype(jnp.bfloat16)
    return lax.dot_general(scaled, weighted, (((1,), (1,)), ((), ())), preferred_element_type=jnp.float32)
```

```python
import functools
import jax
import jax.numpy as jnp
from jax import lax
from jax.experimental import pallas as pl
from jax.experimental.pallas import tpu as pltpu
from jax.sharding import PartitionSpec as P

MESH = pl.DeviceIdType.MESH
VMEM_BUDGET = 56 * 1024 * 1024


def weigh_rows(row_period, row_site, period_err, site_err):
    period_hit = row_period[:, None] == jnp.arange(period_err.shape[0], dtype=jnp.int32)[None, :]
    site_hit = row_site[:, None] == jnp.arange(site_err.shape[0], dtype=jnp.int32)[None, :]
    period_scale = jnp.sum(jnp.where(period_hit, period_err[None, :], 0.0), axis=1)
    site_scale = jnp.sum(jnp.where(site_hit, site_err[None, :], 0.0), axis=1)
    return 1.0 / jnp.sqrt(period_scale * period_scale + site_scale * site_scale)


def pack_rows(sensitivity, row_period, row_site, period_err, site_err):
    row_weight = weigh_rows(row_period, row_site, period_err, site_err)
    return (row_weight[:, None] * sensitivity).astype(jnp.bfloat16)


def weigh_columns(scaled, cell_var, cell_perm, first_cell):
    width = scaled.shape[1]
    positions = lax.dynamic_slice_in_dim(cell_perm, first_cell, width)
    column_var = cell_var[positions]
    return (scaled.astype(jnp.float32) * column_var[None, :]).astype(jnp.bfloat16)


def against(rows_block, weighted):
    return lax.dot_general(
        rows_block, weighted, (((1,), (1,)), ((), ())), preferred_element_type=jnp.float32
    )


def body_general(sensitivity, row_period, row_site, period_err, site_err, cell_var, cell_perm):
    packed = pack_rows(sensitivity, row_period, row_site, period_err, site_err)
    total_cells = cell_var.shape[0]
    scaled = lax.all_to_all(packed, "cell", split_axis=1, concat_axis=0, tiled=True)
    first_cell = lax.axis_index("cell") * (total_cells // lax.axis_size("cell"))
    weighted = weigh_columns(scaled, cell_var, cell_perm, first_cell)
    partial_value = against(lax.all_gather(scaled, "dp", axis=0, tiled=True), weighted)
    gram = lax.psum_scatter(partial_value, "cell", scatter_dimension=0, tiled=True)
    return gram


def flip(index, mask):
    bit = 1
    while bit <= mask:
        if mask & bit:
            index = index + (1 - 2 * ((index // bit) % 2)) * bit
        bit *= 2
    return index


def subsets(bits):
    masks = [0]
    for bit in bits:
        masks = masks + [mask | (1 << bit) for mask in masks]
    return masks


def halvings(n_cell):
    levels = n_cell.bit_length() - 1
    rest = list(range(1, levels))
    orders = (rest, rest[::-1])
    rounds = [[(0, rest, None)]]
    for depth in range(len(rest)):
        rounds.append([(order[depth], order[depth + 1:], half) for half, order in enumerate(orders)])
    return rounds


def gram_kernel(
    n_dp, n_cell,
    sens_ref, weight_ref, perm_ref, table_ref, out_ref,
    stage, outgoing, rows, weighted, column_var, partial, *rest,
):
    rounds = halvings(n_cell)
    n_bufs = sum(len(steps) for steps in rounds)
    bufs, (z_buf, load_sem, send_sem, recv_sem, rs_send, rs_recv, z_send, z_recv) = rest[:n_bufs], rest[n_bufs:]
    dp, cell = lax.axis_index("dp"), lax.axis_index("cell")
    n_rows, n_all = sens_ref.shape
    width = n_all // (n_dp * n_cell)
    plane = n_cell * n_rows
    n_total = n_dp * plane
    send_order = sorted(range(n_dp), key=lambda m: (m == 0, -m))

    barrier = pltpu.get_barrier_semaphore()
    for m in range(n_dp):
        for c in range(n_cell):
            if m or c:
                pl.semaphore_signal(barrier, inc=1, device_id=(flip(dp, m), flip(cell, c)), device_id_type=MESH)

    def load(m):
        first = pl.multiple_of(flip(dp, m) * (n_cell * width), 128)
        return pltpu.make_async_copy(sens_ref.at[:, pl.ds(first, n_cell * width)], stage.at[m], load_sem.at[m])

    for m in send_order:
        load(m).start()

    def transfer(m, c):
        return pltpu.make_async_remote_copy(
            src_ref=outgoing.at[m, c],
            dst_ref=rows.at[dp * n_cell + cell],
            send_sem=send_sem.at[m, c],
            recv_sem=recv_sem.at[m, c],
            device_id=(flip(dp, m), flip(cell, c)),
            device_id_type=MESH,
        )

    def arrival(m, c):
        return pltpu.make_async_remote_copy(
            src_ref=outgoing.at[m, c],
            dst_ref=rows.at[flip(dp, m) * n_cell + flip(cell, c)],
            send_sem=send_sem.at[m, c],
            recv_sem=recv_sem.at[m, c],
            device_id=(flip(dp, m), flip(cell, c)),
            device_id_type=MESH,
        )

    weight = weight_ref[...]
    for place, m in enumerate(send_order):
        load(m).wait()
        for c in reversed(range(n_cell)):
            first = pl.multiple_of(flip(cell, c) * width, 128)
            block = (weight * stage[m, :, pl.ds(first, width)]).astype(jnp.bfloat16)
            if m or c:
                outgoing[m, c] = block
            else:
                rows[dp * n_cell + cell] = block
            if place == 0 and c == n_cell - 1:
                pl.semaphore_wait(barrier, n_dp * n_cell - 1)
            if m or c:
                transfer(m, c).start()

    table = table_ref[...]
    high = table.astype(jnp.bfloat16)
    left = table - high.astype(jnp.float32)
    middle = left.astype(jnp.bfloat16)
    low = (left - middle.astype(jnp.float32)).astype(jnp.bfloat16)
    t_rows, t_cols = table.shape
    tile = min(width, 512)

    @pl.loop(0, width // tile)
    def _(i):
        at = pl.ds(pl.multiple_of(i * tile, 128), tile)
        where = perm_ref[:, at]
        hit = (lax.broadcasted_iota(jnp.int32, (t_cols, tile), 0) == where % t_cols)
        hit = jnp.where(hit, 1.0, 0.0).astype(jnp.bfloat16)
        found = jnp.dot(high, hit, preferred_element_type=jnp.float32)
        found = found + jnp.dot(middle, hit, preferred_element_type=jnp.float32)
        found = found + jnp.dot(low, hit, preferred_element_type=jnp.float32)
        mine = lax.broadcasted_iota(jnp.int32, (t_rows, tile), 0) == where // t_cols
        column_var[:, at] = jnp.sum(jnp.where(mine, found, 0.0), axis=0, keepdims=True)

    for m in range(n_dp):
        group = flip(dp, m)
        for c in range(n_cell):
            if m or c:
                arrival(m, c).wait_recv()

        @pl.loop(0, n_cell)
        def _(c):
            block = rows[group * n_cell + c].astype(jnp.float32) * column_var[...]
            weighted[group * n_cell + c] = block.astype(jnp.bfloat16)

        def product(a, b):
            left_rows = rows[pl.ds(a * n_cell, n_cell)].reshape(plane, width)
            right_rows = weighted[pl.ds(b * n_cell, n_cell)].reshape(plane, width)
            at_row = pl.ds(pl.multiple_of(a * plane, plane), plane)
            at_col = pl.ds(pl.multiple_of(b * plane, plane), plane)
            partial[at_row, at_col] = against(left_rows, right_rows)

        product(group, group)
        for other in range(m):
            product(group, flip(dp, other))
            product(flip(dp, other), group)

    part = n_total // n_cell
    index = 0
    for steps in rounds:
        pending = []
        for bit, left_bits, half in steps:
            n_cols = n_total if half is None else n_total // 2
            cols = pl.ds(0 if half is None else half * n_cols, n_cols)
            for slot, sub in enumerate(subsets(left_bits)):
                there = pl.ds(pl.multiple_of(flip(cell, (1 << bit) ^ sub) * part, part), part)
                here = pl.ds(pl.multiple_of(flip(cell, sub) * part, part), part)
                copy = pltpu.make_async_remote_copy(
                    src_ref=partial.at[there, cols],
                    dst_ref=bufs[index].at[slot],
                    send_sem=rs_send.at[index, slot],
                    recv_sem=rs_recv.at[index, slot],
                    device_id=(dp, flip(cell, 1 << bit)),
                    device_id_type=MESH,
                )
                copy.start()
                pending.append((copy, index, slot, here, cols))
            index += 1
        for copy, at, slot, here, cols in pending:
            copy.wait_recv()
            partial[here, cols] += bufs[at][slot]
        for copy, *_ in pending:
            copy.wait_send()

    mine = pl.ds(pl.multiple_of(cell * part, part), part)
    out_cols = n_total // n_dp

    def columns_of(index):
        return pl.ds(pl.multiple_of(index * out_cols, out_cols), out_cols)

    last = []
    for m in reversed(range(1, n_dp)):
        copy = pltpu.make_async_remote_copy(
            src_ref=partial.at[mine, columns_of(flip(dp, m))],
            dst_ref=z_buf.at[m],
            send_sem=z_send.at[m],
            recv_sem=z_recv.at[m],
            device_id=(flip(dp, m), cell),
            device_id_type=MESH,
        )
        copy.start()
        last.append((copy, m))
    total = partial[mine, columns_of(dp)]
    for copy, m in reversed(last):
        copy.wait_recv()
        total = total + z_buf[m]
    out_ref[...] = total
    for copy, m in last:
        copy.wait_send()
    for m in range(n_dp):
        for c in range(n_cell):
            if m or c:
                transfer(m, c).wait_send()


def body_vmem(sensitivity, row_period, row_site, period_err, site_err, cell_var, cell_perm):
    n_dp, n_cell = lax.axis_size("dp"), lax.axis_size("cell")
    n_rows, n_all = sensitivity.shape
    width = n_all // (n_dp * n_cell)
    n_total = n_rows * n_dp * n_cell
    part = n_total // n_cell
    weight = weigh_rows(row_period, row_site, period_err, site_err)[:, None]
    me = lax.axis_index("dp") * n_cell + lax.axis_index("cell")
    perm = lax.dynamic_slice_in_dim(cell_perm, me * width, width)[None, :]
    t_cols = min(512, n_all)
    table = cell_var.reshape(n_all // t_cols, t_cols)
    bufs = []
    for steps in halvings(n_cell):
        for _, left_bits, half in steps:
            n_cols = n_total if half is None else n_total // 2
            bufs.append(pltpu.VMEM((1 << len(left_bits), part, n_cols), jnp.float32))
    n_bufs, n_slots = len(bufs), n_cell // 2
    vmem = pl.BlockSpec(memory_space=pltpu.VMEM)
    return pl.pallas_call(
        functools.partial(gram_kernel, n_dp, n_cell),
        out_shape=jax.ShapeDtypeStruct((part, n_total // n_dp), jnp.float32),
        in_specs=[pl.BlockSpec(memory_space=pl.ANY), vmem, vmem, vmem],
        out_specs=vmem,
        scratch_shapes=[
            pltpu.VMEM((n_dp, n_rows, n_cell * width), jnp.float32),
            pltpu.VMEM((n_dp, n_cell, n_rows, width), jnp.bfloat16),
            pltpu.VMEM((n_dp * n_cell, n_rows, width), jnp.bfloat16),
            pltpu.VMEM((n_dp * n_cell, n_rows, width), jnp.bfloat16),
            pltpu.VMEM((1, width), jnp.float32),
            pltpu.VMEM((n_total, n_total), jnp.float32),
            *bufs,
            pltpu.VMEM((n_dp, part, n_total // n_dp), jnp.float32),
            pltpu.SemaphoreType.DMA((n_dp,)),
            pltpu.SemaphoreType.DMA((n_dp, n_cell)),
            pltpu.SemaphoreType.DMA((n_dp, n_cell)),
            pltpu.SemaphoreType.DMA((n_bufs, n_slots)),
            pltpu.SemaphoreType.DMA((n_bufs, n_slots)),
            pltpu.SemaphoreType.DMA((n_dp,)),
            pltpu.SemaphoreType.DMA((n_dp,)),
        ],
        compiler_params=pltpu.CompilerParams(
            collective_id=0, has_side_effects=True, vmem_limit_bytes=VMEM_BUDGET
        ),
        cost_estimate=pl.CostEstimate(
            flops=2 * n_total * n_total * width, bytes_accessed=4 * n_rows * n_all, transcendentals=0
        ),
    )(sensitivity, weight, perm, table)


def is_power_of_two(n):
    return n & (n - 1) == 0


def body(*arrays):
    sensitivity = arrays[0]
    n_dp, n_cell = lax.axis_size("dp"), lax.axis_size("cell")
    n_rows, n_all = sensitivity.shape
    n_total = n_rows * n_dp * n_cell
    need = (4 + 2 + 2 + 2) * n_rows * n_all + 2 * 4 * n_total * n_total
    fits = need < VMEM_BUDGET and is_power_of_two(n_dp) and is_power_of_two(n_cell) and n_cell > 1
    return (body_vmem if fits else body_general)(*arrays)


def solution(mesh):
    return jax.shard_map(
        body,
        mesh=mesh,
        in_specs=(
            P(("dp", "cell"), None),
            P(("dp", "cell")),
            P(("dp", "cell")),
            P(),
            P(),
            P(),
            P(),
        ),
        out_specs=P("cell", "dp"),
        check_vma=False,
    )
```

```python
import functools
import jax
import jax.numpy as jnp
from jax import lax
from jax.experimental import pallas as pl
from jax.experimental.pallas import tpu as pltpu
from jax.sharding import PartitionSpec as P

MESH = pl.DeviceIdType.MESH
VMEM_BUDGET = 56 * 1024 * 1024
PIECES = 4


def weigh_rows(row_period, row_site, period_err, site_err):
    period_hit = row_period[:, None] == jnp.arange(period_err.shape[0], dtype=jnp.int32)[None, :]
    site_hit = row_site[:, None] == jnp.arange(site_err.shape[0], dtype=jnp.int32)[None, :]
    period_scale = jnp.sum(jnp.where(period_hit, period_err[None, :], 0.0), axis=1)
    site_scale = jnp.sum(jnp.where(site_hit, site_err[None, :], 0.0), axis=1)
    return 1.0 / jnp.sqrt(period_scale * period_scale + site_scale * site_scale)


def pack_rows(sensitivity, row_period, row_site, period_err, site_err):
    row_weight = weigh_rows(row_period, row_site, period_err, site_err)
    return (row_weight[:, None] * sensitivity).astype(jnp.bfloat16)


def weigh_columns(scaled, cell_var, cell_perm, first_cell):
    width = scaled.shape[1]
    positions = lax.dynamic_slice_in_dim(cell_perm, first_cell, width)
    column_var = cell_var[positions]
    return (scaled.astype(jnp.float32) * column_var[None, :]).astype(jnp.bfloat16)


def against(rows_block, weighted):
    return lax.dot_general(
        rows_block, weighted, (((1,), (1,)), ((), ())), preferred_element_type=jnp.float32
    )


def body_general(sensitivity, row_period, row_site, period_err, site_err, cell_var, cell_perm):
    packed = pack_rows(sensitivity, row_period, row_site, period_err, site_err)
    total_cells = cell_var.shape[0]
    scaled = lax.all_to_all(packed, "cell", split_axis=1, concat_axis=0, tiled=True)
    first_cell = lax.axis_index("cell") * (total_cells // lax.axis_size("cell"))
    weighted = weigh_columns(scaled, cell_var, cell_perm, first_cell)
    partial_value = against(lax.all_gather(scaled, "dp", axis=0, tiled=True), weighted)
    gram = lax.psum_scatter(partial_value, "cell", scatter_dimension=0, tiled=True)
    return gram


def flip(index, mask):
    bit = 1
    while bit <= mask:
        if mask & bit:
            index = index + (1 - 2 * ((index // bit) % 2)) * bit
        bit *= 2
    return index


def subsets(bits):
    masks = [0]
    for bit in bits:
        masks = masks + [mask | (1 << bit) for mask in masks]
    return masks


def halvings(n_dp, n_cell):
    levels = n_cell.bit_length() - 1
    rest = list(range(1, levels))
    orders = (rest, rest[::-1])
    rounds = [[("cell", 0, rest, None, jnp.float32)]]
    for depth in range(len(rest)):
        rounds.append([
            ("cell", order[depth], order[depth + 1:], half, jnp.bfloat16) for half, order in enumerate(orders)
        ])
    dp_levels = n_dp.bit_length() - 1
    for bit in range(dp_levels):
        rounds.append([("dp", bit, list(range(bit + 1, dp_levels)), None, jnp.float32)])
    return rounds


def step_shape(step, n_dp, n_cell, n_total):
    axis, _, left_bits, half, _ = step
    n_cols = n_total // n_dp if axis == "dp" else n_total if half is None else n_total // 2
    return (PIECES, 1 << len(left_bits), n_total // n_cell // PIECES, n_cols)


def gram_kernel(
    n_dp, n_cell,
    sens_ref, weight_ref, perm_ref, table_ref, out_ref,
    stage, outgoing, rows, weighted, column_var, partial, *rest,
):
    rounds = halvings(n_dp, n_cell)
    flat = [step for steps in rounds for step in steps]
    rest = list(rest)
    arrived = [rest.pop(0) for _ in flat]
    leaving = [rest.pop(0) if step[-1] != jnp.float32 else None for step in flat]
    load_sem, send_sem, recv_sem, sum_send, sum_recv = rest
    dp, cell = lax.axis_index("dp"), lax.axis_index("cell")
    n_rows, n_all = sens_ref.shape
    width = n_all // (n_dp * n_cell)
    plane = n_cell * n_rows
    n_total = n_dp * plane
    top = n_dp // 2
    early = [m for m in reversed(range(n_dp)) if m != top]
    send_order = [(m, c) for c in reversed(range(n_cell)) for m in early]
    if top:
        send_order += [(top, c) for c in reversed(range(n_cell))]
    group_order = sorted(range(n_dp), key=lambda m: (m == top, m))

    barrier = pltpu.get_barrier_semaphore()
    for m in range(n_dp):
        for c in range(n_cell):
            if m or c:
                pl.semaphore_signal(barrier, inc=1, device_id=(flip(dp, m), flip(cell, c)), device_id_type=MESH)

    def load(m, c):
        first = pl.multiple_of((flip(dp, m) * n_cell + flip(cell, c)) * width, 128)
        return pltpu.make_async_copy(sens_ref.at[:, pl.ds(first, width)], stage.at[m, c], load_sem.at[m, c])

    for m, c in send_order:
        load(m, c).start()

    def transfer(m, c):
        return pltpu.make_async_remote_copy(
            src_ref=outgoing.at[m, c],
            dst_ref=rows.at[dp * n_cell + cell],
            send_sem=send_sem.at[m, c],
            recv_sem=recv_sem.at[m, c],
            device_id=(flip(dp, m), flip(cell, c)),
            device_id_type=MESH,
        )

    def arrival(m, c):
        return pltpu.make_async_remote_copy(
            src_ref=outgoing.at[m, c],
            dst_ref=rows.at[flip(dp, m) * n_cell + flip(cell, c)],
            send_sem=send_sem.at[m, c],
            recv_sem=recv_sem.at[m, c],
            device_id=(flip(dp, m), flip(cell, c)),
            device_id_type=MESH,
        )

    weight = weight_ref[...]
    for place, (m, c) in enumerate(send_order):
        load(m, c).wait()
        block = (weight * stage[m, c]).astype(jnp.bfloat16)
        if m or c:
            outgoing[m, c] = block
        else:
            rows[dp * n_cell + cell] = block
        if place == 0:
            pl.semaphore_wait(barrier, n_dp * n_cell - 1)
        if m or c:
            transfer(m, c).start()

    table = table_ref[...]
    high = table.astype(jnp.bfloat16)
    left = table - high.astype(jnp.float32)
    middle = left.astype(jnp.bfloat16)
    low = (left - middle.astype(jnp.float32)).astype(jnp.bfloat16)
    t_rows, t_cols = table.shape
    tile = min(width, 512)

    @pl.loop(0, width // tile)
    def _(i):
        at = pl.ds(pl.multiple_of(i * tile, 128), tile)
        where = perm_ref[:, at]
        hit = (lax.broadcasted_iota(jnp.int32, (t_cols, tile), 0) == where % t_cols)
        hit = jnp.where(hit, 1.0, 0.0).astype(jnp.bfloat16)
        found = jnp.dot(high, hit, preferred_element_type=jnp.float32)
        found = found + jnp.dot(middle, hit, preferred_element_type=jnp.float32)
        found = found + jnp.dot(low, hit, preferred_element_type=jnp.float32)
        mine = lax.broadcasted_iota(jnp.int32, (t_rows, tile), 0) == where // t_cols
        column_var[:, at] = jnp.sum(jnp.where(mine, found, 0.0), axis=0, keepdims=True)

    for place, m in enumerate(group_order):
        group = flip(dp, m)
        for c in range(n_cell):
            if m or c:
                arrival(m, c).wait_recv()

        @pl.loop(0, n_cell)
        def _(c):
            block = rows[group * n_cell + c].astype(jnp.float32) * column_var[...]
            weighted[group * n_cell + c] = block.astype(jnp.bfloat16)

        def product(a, b):
            left_rows = rows[pl.ds(a * n_cell, n_cell)].reshape(plane, width)
            right_rows = weighted[pl.ds(b * n_cell, n_cell)].reshape(plane, width)
            at_row = pl.ds(pl.multiple_of(a * plane, plane), plane)
            at_col = pl.ds(pl.multiple_of(b * plane, plane), plane)
            partial[at_row, at_col] = against(left_rows, right_rows)

        product(group, group)
        for other in group_order[:place]:
            product(group, flip(dp, other))
            product(flip(dp, other), group)

    part, out_cols = n_total // n_cell, n_total // n_dp
    piece_rows = part // PIECES
    numbers, count = [], 0
    for steps in rounds:
        numbers.append(list(range(count, count + len(steps))))
        count += len(steps)

    def rows_of(block, piece):
        return pl.ds(pl.multiple_of(block * part + piece * piece_rows, piece_rows), piece_rows)

    def columns_of(index):
        return pl.ds(pl.multiple_of(index * out_cols, out_cols), out_cols)

    def exchanges(number, piece):
        axis, bit, left_bits, half, kind = flat[number]
        found = []
        for slot, sub in enumerate(subsets(left_bits)):
            if axis == "cell":
                n_cols = n_total if half is None else n_total // 2
                cols = pl.ds(0 if half is None else half * n_cols, n_cols)
                there = (rows_of(flip(cell, (1 << bit) ^ sub), piece), cols)
                here = (rows_of(flip(cell, sub), piece), cols)
                device = (dp, flip(cell, 1 << bit))
            else:
                mine = rows_of(cell, piece)
                there = (mine, columns_of(flip(dp, (1 << bit) ^ sub)))
                here = (mine, columns_of(flip(dp, sub)))
                device = (flip(dp, 1 << bit), cell)
            source = partial.at[there] if kind == jnp.float32 else leaving[number].at[piece, slot]
            copy = pltpu.make_async_remote_copy(
                src_ref=source,
                dst_ref=arrived[number].at[piece, slot],
                send_sem=sum_send.at[number, piece, slot],
                recv_sem=sum_recv.at[number, piece, slot],
                device_id=device,
                device_id_type=MESH,
            )
            found.append((copy, slot, there, here))
        return found

    def begin(steps, piece):
        for number in steps:
            for copy, slot, there, _ in exchanges(number, piece):
                if leaving[number] is not None:
                    leaving[number][piece, slot] = partial[there].astype(leaving[number].dtype)
                copy.start()

    def finish(steps, piece):
        for number in steps:
            for copy, slot, _, here in exchanges(number, piece):
                copy.wait_recv()
                partial[here] += arrived[number][piece, slot].astype(jnp.float32)

    for depth, steps in enumerate(numbers):
        for piece in range(PIECES):
            if depth:
                finish(numbers[depth - 1], piece)
            begin(steps, piece)
    for piece in range(PIECES):
        finish(numbers[-1], piece)
        out_ref[pl.ds(piece * piece_rows, piece_rows)] = partial[rows_of(cell, piece), columns_of(dp)]

    for number in range(count):
        for piece in range(PIECES):
            for copy, *_ in exchanges(number, piece):
                copy.wait_send()
    for m in range(n_dp):
        for c in range(n_cell):
            if m or c:
                transfer(m, c).wait_send()


def body_vmem(sensitivity, row_period, row_site, period_err, site_err, cell_var, cell_perm):
    n_dp, n_cell = lax.axis_size("dp"), lax.axis_size("cell")
    n_rows, n_all = sensitivity.shape
    width = n_all // (n_dp * n_cell)
    n_total = n_rows * n_dp * n_cell
    part = n_total // n_cell
    weight = weigh_rows(row_period, row_site, period_err, site_err)[:, None]
    me = lax.axis_index("dp") * n_cell + lax.axis_index("cell")
    perm = lax.dynamic_slice_in_dim(cell_perm, me * width, width)[None, :]
    t_cols = min(512, n_all)
    table = cell_var.reshape(n_all // t_cols, t_cols)
    flat = [step for steps in halvings(n_dp, n_cell) for step in steps]
    bufs = [pltpu.VMEM(step_shape(step, n_dp, n_cell, n_total), step[-1]) for step in flat]
    bufs += [
        pltpu.VMEM(step_shape(step, n_dp, n_cell, n_total), step[-1]) for step in flat if step[-1] != jnp.float32
    ]
    sums = (len(flat), PIECES, n_cell // 2 + n_dp // 2)
    vmem = pl.BlockSpec(memory_space=pltpu.VMEM)
    return pl.pallas_call(
        functools.partial(gram_kernel, n_dp, n_cell),
        out_shape=jax.ShapeDtypeStruct((part, n_total // n_dp), jnp.float32),
        in_specs=[pl.BlockSpec(memory_space=pl.ANY), vmem, vmem, vmem],
        out_specs=vmem,
        scratch_shapes=[
            pltpu.VMEM((n_dp, n_cell, n_rows, width), jnp.float32),
            pltpu.VMEM((n_dp, n_cell, n_rows, width), jnp.bfloat16),
            pltpu.VMEM((n_dp * n_cell, n_rows, width), jnp.bfloat16),
            pltpu.VMEM((n_dp * n_cell, n_rows, width), jnp.bfloat16),
            pltpu.VMEM((1, width), jnp.float32),
            pltpu.VMEM((n_total, n_total), jnp.float32),
            *bufs,
            pltpu.SemaphoreType.DMA((n_dp, n_cell)),
            pltpu.SemaphoreType.DMA((n_dp, n_cell)),
            pltpu.SemaphoreType.DMA((n_dp, n_cell)),
            pltpu.SemaphoreType.DMA(sums),
            pltpu.SemaphoreType.DMA(sums),
        ],
        compiler_params=pltpu.CompilerParams(
            collective_id=0, has_side_effects=True, vmem_limit_bytes=VMEM_BUDGET
        ),
        cost_estimate=pl.CostEstimate(
            flops=2 * n_total * n_total * width, bytes_accessed=4 * n_rows * n_all, transcendentals=0
        ),
    )(sensitivity, weight, perm, table)


def is_power_of_two(n):
    return n & (n - 1) == 0


def body(*arrays):
    sensitivity = arrays[0]
    n_dp, n_cell = lax.axis_size("dp"), lax.axis_size("cell")
    n_rows, n_all = sensitivity.shape
    n_total = n_rows * n_dp * n_cell
    need = (4 + 2 + 2 + 2) * n_rows * n_all + 2 * 4 * n_total * n_total
    fits = n_total // n_cell % (16 * PIECES) == 0 and need < VMEM_BUDGET and is_power_of_two(n_dp) and is_power_of_two(n_cell) and n_cell > 1
    return (body_vmem if fits else body_general)(*arrays)


def solution(mesh):
    return jax.shard_map(
        body,
        mesh=mesh,
        in_specs=(
            P(("dp", "cell"), None),
            P(("dp", "cell")),
            P(("dp", "cell")),
            P(),
            P(),
            P(),
            P(),
        ),
        out_specs=P("cell", "dp"),
        check_vma=False,
    )
```

```python
import functools
import jax
import jax.numpy as jnp
from jax import lax
from jax.experimental import pallas as pl
from jax.experimental.pallas import tpu as pltpu
from jax.sharding import PartitionSpec as P

MESH = pl.DeviceIdType.MESH
VMEM_BUDGET = 56 * 1024 * 1024
PIECES = 4
CHUNKS = 4


def weigh_rows(row_period, row_site, period_err, site_err):
    period_hit = row_period[:, None] == jnp.arange(period_err.shape[0], dtype=jnp.int32)[None, :]
    site_hit = row_site[:, None] == jnp.arange(site_err.shape[0], dtype=jnp.int32)[None, :]
    period_scale = jnp.sum(jnp.where(period_hit, period_err[None, :], 0.0), axis=1)
    site_scale = jnp.sum(jnp.where(site_hit, site_err[None, :], 0.0), axis=1)
    return 1.0 / jnp.sqrt(period_scale * period_scale + site_scale * site_scale)


def pack_rows(sensitivity, row_period, row_site, period_err, site_err):
    row_weight = weigh_rows(row_period, row_site, period_err, site_err)
    return (row_weight[:, None] * sensitivity).astype(jnp.bfloat16)


def weigh_columns(scaled, cell_var, cell_perm, first_cell):
    width = scaled.shape[1]
    positions = lax.dynamic_slice_in_dim(cell_perm, first_cell, width)
    column_var = cell_var[positions]
    return (scaled.astype(jnp.float32) * column_var[None, :]).astype(jnp.bfloat16)


def against(rows_block, weighted):
    return lax.dot_general(
        rows_block, weighted, (((1,), (1,)), ((), ())), preferred_element_type=jnp.float32
    )


def body_general(sensitivity, row_period, row_site, period_err, site_err, cell_var, cell_perm):
    packed = pack_rows(sensitivity, row_period, row_site, period_err, site_err)
    total_cells = cell_var.shape[0]
    scaled = lax.all_to_all(packed, "cell", split_axis=1, concat_axis=0, tiled=True)
    first_cell = lax.axis_index("cell") * (total_cells // lax.axis_size("cell"))
    weighted = weigh_columns(scaled, cell_var, cell_perm, first_cell)
    partial_value = against(lax.all_gather(scaled, "dp", axis=0, tiled=True), weighted)
    gram = lax.psum_scatter(partial_value, "cell", scatter_dimension=0, tiled=True)
    return gram


def flip(index, mask):
    bit = 1
    while bit <= mask:
        if mask & bit:
            index = index + (1 - 2 * ((index // bit) % 2)) * bit
        bit *= 2
    return index


def subsets(bits):
    masks = [0]
    for bit in bits:
        masks = masks + [mask | (1 << bit) for mask in masks]
    return masks


def halvings(n_dp, n_cell):
    levels = n_cell.bit_length() - 1
    rest = list(range(1, levels))
    orders = (rest, rest[::-1])
    rounds = [[("cell", 0, rest, None, jnp.float32)]]
    for depth in range(len(rest)):
        rounds.append([
            ("cell", order[depth], order[depth + 1:], half, jnp.float32) for half, order in enumerate(orders)
        ])
    dp_levels = n_dp.bit_length() - 1
    for bit in range(dp_levels):
        rounds.append([("dp", bit, list(range(bit + 1, dp_levels)), None, jnp.float32)])
    return rounds


def step_shape(step, n_dp, n_cell, n_total):
    axis, _, left_bits, half, _ = step
    n_cols = n_total // n_dp if axis == "dp" else n_total if half is None else n_total // 2
    return (PIECES, 1 << len(left_bits), n_total // n_cell // PIECES, n_cols)


def gram_kernel(
    n_dp, n_cell,
    sens_ref, weight_ref, perm_ref, var_ref, out_ref,
    stage, outgoing, rows, weighted, perm, flat_table, table, column_var, partial, *rest,
):
    rounds = halvings(n_dp, n_cell)
    flat = [step for steps in rounds for step in steps]
    rest = list(rest)
    arrived = [rest.pop(0) for _ in flat]
    leaving = [rest.pop(0) if step[-1] != jnp.float32 else None for step in flat]
    load_sem, small_sem, send_sem, recv_sem, sum_send, sum_recv = rest
    dp, cell = lax.axis_index("dp"), lax.axis_index("cell")
    n_rows, n_all = sens_ref.shape
    width = n_all // (n_dp * n_cell)
    plane = n_cell * n_rows
    n_total = n_dp * plane
    chunk_width = width // CHUNKS
    far = [m for m in reversed(range(n_dp)) if m >= n_dp // 2]
    near = [m for m in reversed(range(n_dp)) if m < n_dp // 2]
    masks = [m for pair in zip(far, near) for m in pair] if near else far
    send_order = [(m, c) for c in reversed(range(n_cell)) for m in masks]

    barrier = pltpu.get_barrier_semaphore()
    for m in range(n_dp):
        for c in range(n_cell):
            if m or c:
                pl.semaphore_signal(barrier, inc=1, device_id=(flip(dp, m), flip(cell, c)), device_id_type=MESH)

    def load(m, c):
        first = pl.multiple_of((flip(dp, m) * n_cell + flip(cell, c)) * width, 128)
        return pltpu.make_async_copy(sens_ref.at[:, pl.ds(first, width)], stage.at[m, c], load_sem.at[m, c])

    for m, c in send_order:
        load(m, c).start()
    me = dp * n_cell + cell
    load_perm = pltpu.make_async_copy(
        perm_ref.at[pl.ds(pl.multiple_of(me * width, width), width)], perm, small_sem.at[0]
    )
    load_var = pltpu.make_async_copy(var_ref, flat_table, small_sem.at[1])
    load_perm.start()
    load_var.start()

    def transfer(chunk, m, c):
        return pltpu.make_async_remote_copy(
            src_ref=outgoing.at[chunk, m, c],
            dst_ref=rows.at[chunk, me],
            send_sem=send_sem.at[chunk, m, c],
            recv_sem=recv_sem.at[chunk, m, c],
            device_id=(flip(dp, m), flip(cell, c)),
            device_id_type=MESH,
        )

    def arrival(chunk, m, c):
        return pltpu.make_async_remote_copy(
            src_ref=outgoing.at[chunk, m, c],
            dst_ref=rows.at[chunk, flip(dp, m) * n_cell + flip(cell, c)],
            send_sem=send_sem.at[chunk, m, c],
            recv_sem=recv_sem.at[chunk, m, c],
            device_id=(flip(dp, m), flip(cell, c)),
            device_id_type=MESH,
        )

    weight = weight_ref[...]
    for chunk in range(CHUNKS):
        for place, (m, c) in enumerate(send_order):
            if chunk == 0:
                load(m, c).wait()
            at = pl.ds(chunk * chunk_width, chunk_width)
            block = (weight * stage[m, c, :, at]).astype(jnp.bfloat16)
            if m or c:
                outgoing[chunk, m, c] = block
            else:
                rows[chunk, me] = block
            if chunk == 0 and place == 0:
                pl.semaphore_wait(barrier, n_dp * n_cell - 1)
            if m or c:
                transfer(chunk, m, c).start()

    load_perm.wait()
    load_var.wait()
    t_rows, t_cols = table.shape

    @pl.loop(0, t_rows)
    def _(i):
        at = pl.ds(pl.multiple_of(i * t_cols, t_cols), t_cols)
        table[pl.ds(i, 1), :] = flat_table[at].reshape(1, t_cols)

    values = table[...]
    high = values.astype(jnp.bfloat16)
    left = values - high.astype(jnp.float32)
    middle = left.astype(jnp.bfloat16)
    low = (left - middle.astype(jnp.float32)).astype(jnp.bfloat16)
    tile = chunk_width

    @pl.loop(0, width // tile)
    def _(i):
        at = pl.ds(pl.multiple_of(i * tile, tile), tile)
        where = perm[at].reshape(1, tile)
        hit = (lax.broadcasted_iota(jnp.int32, (t_cols, tile), 0) == where % t_cols)
        hit = jnp.where(hit, 1.0, 0.0).astype(jnp.bfloat16)
        found = jnp.dot(high, hit, preferred_element_type=jnp.float32)
        found = found + jnp.dot(middle, hit, preferred_element_type=jnp.float32)
        found = found + jnp.dot(low, hit, preferred_element_type=jnp.float32)
        mine = lax.broadcasted_iota(jnp.int32, (t_rows, tile), 0) == where // t_cols
        column_var[i] = jnp.sum(jnp.where(mine, found, 0.0), axis=0, keepdims=True)

    for chunk in range(CHUNKS):
        for m, c in send_order:
            if m or c:
                arrival(chunk, m, c).wait_recv()

        @pl.loop(0, n_dp)
        def _(group):
            first = group * n_cell

            @pl.loop(0, n_cell)
            def _(c):
                block = rows[chunk, first + c].astype(jnp.float32) * column_var[chunk]
                weighted[first + c] = block.astype(jnp.bfloat16)

            right_rows = weighted[pl.ds(first, n_cell)].reshape(plane, chunk_width)
            left_rows = rows[chunk].reshape(n_total, chunk_width)
            cols = pl.ds(pl.multiple_of(group * plane, plane), plane)
            term = against(left_rows, right_rows)
            if chunk == 0:
                partial[:, cols] = term
            else:
                partial[:, cols] += term

    part, out_cols = n_total // n_cell, n_total // n_dp
    piece_rows = part // PIECES
    numbers, count = [], 0
    for steps in rounds:
        numbers.append(list(range(count, count + len(steps))))
        count += len(steps)

    def rows_of(block, piece):
        return pl.ds(pl.multiple_of(block * part + piece * piece_rows, piece_rows), piece_rows)

    def columns_of(index):
        return pl.ds(pl.multiple_of(index * out_cols, out_cols), out_cols)

    def exchanges(number, piece):
        axis, bit, left_bits, half, kind = flat[number]
        found = []
        for slot, sub in enumerate(subsets(left_bits)):
            if axis == "cell":
                n_cols = n_total if half is None else n_total // 2
                cols = pl.ds(0 if half is None else half * n_cols, n_cols)
                there = (rows_of(flip(cell, (1 << bit) ^ sub), piece), cols)
                here = (rows_of(flip(cell, sub), piece), cols)
                device = (dp, flip(cell, 1 << bit))
            else:
                mine = rows_of(cell, piece)
                there = (mine, columns_of(flip(dp, (1 << bit) ^ sub)))
                here = (mine, columns_of(flip(dp, sub)))
                device = (flip(dp, 1 << bit), cell)
            source = partial.at[there] if kind == jnp.float32 else leaving[number].at[piece, slot]
            copy = pltpu.make_async_remote_copy(
                src_ref=source,
                dst_ref=arrived[number].at[piece, slot],
                send_sem=sum_send.at[number, piece, slot],
                recv_sem=sum_recv.at[number, piece, slot],
                device_id=device,
                device_id_type=MESH,
            )
            found.append((copy, slot, there, here))
        return found

    def begin(steps, piece):
        for number in steps:
            for copy, slot, there, _ in exchanges(number, piece):
                if leaving[number] is not None:
                    leaving[number][piece, slot] = partial[there].astype(leaving[number].dtype)
                copy.start()

    def finish(steps, piece):
        for number in steps:
            for copy, slot, _, here in exchanges(number, piece):
                copy.wait_recv()
                partial[here] += arrived[number][piece, slot].astype(jnp.float32)

    for depth, steps in enumerate(numbers):
        for piece in range(PIECES):
            if depth:
                finish(numbers[depth - 1], piece)
            begin(steps, piece)
    for piece in range(PIECES):
        finish(numbers[-1], piece)
        out_ref[pl.ds(piece * piece_rows, piece_rows)] = partial[rows_of(cell, piece), columns_of(dp)]

    for number in range(count):
        for piece in range(PIECES):
            for copy, *_ in exchanges(number, piece):
                copy.wait_send()
    for chunk in range(CHUNKS):
        for m, c in send_order:
            if m or c:
                transfer(chunk, m, c).wait_send()


def body_vmem(sensitivity, row_period, row_site, period_err, site_err, cell_var, cell_perm):
    n_dp, n_cell = lax.axis_size("dp"), lax.axis_size("cell")
    n_rows, n_all = sensitivity.shape
    width = n_all // (n_dp * n_cell)
    n_total = n_rows * n_dp * n_cell
    part = n_total // n_cell
    weight = weigh_rows(row_period, row_site, period_err, site_err)[:, None]
    t_cols = min(512, n_all)
    flat = [step for steps in halvings(n_dp, n_cell) for step in steps]
    bufs = [pltpu.VMEM(step_shape(step, n_dp, n_cell, n_total), step[-1]) for step in flat]
    bufs += [
        pltpu.VMEM(step_shape(step, n_dp, n_cell, n_total), step[-1]) for step in flat if step[-1] != jnp.float32
    ]
    sums = (len(flat), PIECES, n_cell // 2 + n_dp // 2)
    hbm, vmem = pl.BlockSpec(memory_space=pl.ANY), pl.BlockSpec(memory_space=pltpu.VMEM)
    chunk_width = width // CHUNKS
    return pl.pallas_call(
        functools.partial(gram_kernel, n_dp, n_cell),
        out_shape=jax.ShapeDtypeStruct((part, n_total // n_dp), jnp.float32),
        in_specs=[hbm, vmem, hbm, hbm],
        out_specs=vmem,
        scratch_shapes=[
            pltpu.VMEM((n_dp, n_cell, n_rows, width), jnp.float32),
            pltpu.VMEM((CHUNKS, n_dp, n_cell, n_rows, chunk_width), jnp.bfloat16),
            pltpu.VMEM((CHUNKS, n_dp * n_cell, n_rows, chunk_width), jnp.bfloat16),
            pltpu.VMEM((n_dp * n_cell, n_rows, chunk_width), jnp.bfloat16),
            pltpu.VMEM((width,), jnp.int32),
            pltpu.VMEM((n_all,), jnp.float32),
            pltpu.VMEM((n_all // t_cols, t_cols), jnp.float32),
            pltpu.VMEM((CHUNKS, 1, chunk_width), jnp.float32),
            pltpu.VMEM((n_total, n_total), jnp.float32),
            *bufs,
            pltpu.SemaphoreType.DMA((n_dp, n_cell)),
            pltpu.SemaphoreType.DMA((2,)),
            pltpu.SemaphoreType.DMA((CHUNKS, n_dp, n_cell)),
            pltpu.SemaphoreType.DMA((CHUNKS, n_dp, n_cell)),
            pltpu.SemaphoreType.DMA(sums),
            pltpu.SemaphoreType.DMA(sums),
        ],
        compiler_params=pltpu.CompilerParams(
            collective_id=0, has_side_effects=True, vmem_limit_bytes=VMEM_BUDGET
        ),
        cost_estimate=pl.CostEstimate(
            flops=2 * n_total * n_total * width, bytes_accessed=4 * n_rows * n_all, transcendentals=0
        ),
    )(sensitivity, weight, cell_perm, cell_var)


def is_power_of_two(n):
    return n & (n - 1) == 0


def body(*arrays):
    sensitivity = arrays[0]
    n_dp, n_cell = lax.axis_size("dp"), lax.axis_size("cell")
    n_rows, n_all = sensitivity.shape
    n_total = n_rows * n_dp * n_cell
    need = (4 + 2 + 2 + 2) * n_rows * n_all + 2 * 4 * n_total * n_total
    width = n_all // (n_dp * n_cell)
    fits = n_total // n_cell % (16 * PIECES) == 0 and width % (128 * CHUNKS) == 0 and need < VMEM_BUDGET and is_power_of_two(n_dp) and is_power_of_two(n_cell) and n_cell > 1
    return (body_vmem if fits else body_general)(*arrays)


def solution(mesh):
    return jax.shard_map(
        body,
        mesh=mesh,
        in_specs=(
            P(("dp", "cell"), None),
            P(("dp", "cell")),
            P(("dp", "cell")),
            P(),
            P(),
            P(),
            P(),
        ),
        out_specs=P("cell", "dp"),
        check_vma=False,
    )
```

```python
import functools
import jax
import jax.numpy as jnp
from jax import lax
from jax.experimental import pallas as pl
from jax.experimental.pallas import tpu as pltpu
from jax.sharding import PartitionSpec as P

MESH = pl.DeviceIdType.MESH
VMEM_BUDGET = 56 * 1024 * 1024
PIECES = 4
CHUNKS = 4


def weigh_rows(row_period, row_site, period_err, site_err):
    period_hit = row_period[:, None] == jnp.arange(period_err.shape[0], dtype=jnp.int32)[None, :]
    site_hit = row_site[:, None] == jnp.arange(site_err.shape[0], dtype=jnp.int32)[None, :]
    period_scale = jnp.sum(jnp.where(period_hit, period_err[None, :], 0.0), axis=1)
    site_scale = jnp.sum(jnp.where(site_hit, site_err[None, :], 0.0), axis=1)
    return 1.0 / jnp.sqrt(period_scale * period_scale + site_scale * site_scale)


def pack_rows(sensitivity, row_period, row_site, period_err, site_err):
    row_weight = weigh_rows(row_period, row_site, period_err, site_err)
    return (row_weight[:, None] * sensitivity).astype(jnp.bfloat16)


def weigh_columns(scaled, cell_var, cell_perm, first_cell):
    width = scaled.shape[1]
    positions = lax.dynamic_slice_in_dim(cell_perm, first_cell, width)
    column_var = cell_var[positions]
    return (scaled.astype(jnp.float32) * column_var[None, :]).astype(jnp.bfloat16)


def against(rows_block, weighted):
    return lax.dot_general(
        rows_block, weighted, (((1,), (1,)), ((), ())), preferred_element_type=jnp.float32
    )


def body_general(sensitivity, row_period, row_site, period_err, site_err, cell_var, cell_perm):
    packed = pack_rows(sensitivity, row_period, row_site, period_err, site_err)
    total_cells = cell_var.shape[0]
    scaled = lax.all_to_all(packed, "cell", split_axis=1, concat_axis=0, tiled=True)
    first_cell = lax.axis_index("cell") * (total_cells // lax.axis_size("cell"))
    weighted = weigh_columns(scaled, cell_var, cell_perm, first_cell)
    partial_value = against(lax.all_gather(scaled, "dp", axis=0, tiled=True), weighted)
    gram = lax.psum_scatter(partial_value, "cell", scatter_dimension=0, tiled=True)
    return gram


def flip(index, mask):
    bit = 1
    while bit <= mask:
        if mask & bit:
            index = index + (1 - 2 * ((index // bit) % 2)) * bit
        bit *= 2
    return index


def subsets(bits):
    masks = [0]
    for bit in bits:
        masks = masks + [mask | (1 << bit) for mask in masks]
    return masks


def halvings(n_dp, n_cell):
    levels = n_cell.bit_length() - 1
    rest = list(range(1, levels))
    orders = (rest, rest[::-1])
    rounds = [[("cell", 0, rest, None, jnp.float32)]]
    for depth in range(len(rest)):
        rounds.append([
            ("cell", order[depth], order[depth + 1:], half, jnp.float32) for half, order in enumerate(orders)
        ])
    dp_levels = n_dp.bit_length() - 1
    for bit in range(dp_levels):
        rounds.append([("dp", bit, list(range(bit + 1, dp_levels)), None, jnp.float32)])
    return rounds


def step_shape(step, n_dp, n_cell, n_total):
    axis, _, left_bits, half, _ = step
    n_cols = n_total // n_dp if axis == "dp" else n_total if half is None else n_total // 2
    return (PIECES, 1 << len(left_bits), n_total // n_cell // PIECES, n_cols)


def gram_kernel(
    n_dp, n_cell,
    sens_ref, period_ref, site_ref, period_err_ref, site_err_ref, perm_ref, var_ref, out_ref,
    stage, outgoing, rows, weighted, perm, flat_table, table, column_var, partial, *rest,
):
    rounds = halvings(n_dp, n_cell)
    flat = [step for steps in rounds for step in steps]
    rest = list(rest)
    arrived = [rest.pop(0) for _ in flat]
    leaving = [rest.pop(0) if step[-1] != jnp.float32 else None for step in flat]
    load_sem, small_sem, send_sem, recv_sem, sum_send, sum_recv = rest
    dp, cell = lax.axis_index("dp"), lax.axis_index("cell")
    n_rows, n_all = sens_ref.shape
    width = n_all // (n_dp * n_cell)
    plane = n_cell * n_rows
    n_total = n_dp * plane
    chunk_width = width // CHUNKS
    far = [m for m in reversed(range(n_dp)) if m >= n_dp // 2]
    near = [m for m in reversed(range(n_dp)) if m < n_dp // 2]
    masks = [m for pair in zip(far, near) for m in pair] if near else far
    spread = [c for low in range(n_cell // 2) for c in (n_cell - 1 - low, low)]
    send_order = [(m, c if m in far else n_cell - 1 - c) for c in spread for m in masks]

    barrier = pltpu.get_barrier_semaphore()
    for m in range(n_dp):
        for c in range(n_cell):
            if m or c:
                pl.semaphore_signal(barrier, inc=1, device_id=(flip(dp, m), flip(cell, c)), device_id_type=MESH)

    def load(m, c):
        first = pl.multiple_of((flip(dp, m) * n_cell + flip(cell, c)) * width, 128)
        return pltpu.make_async_copy(sens_ref.at[:, pl.ds(first, width)], stage.at[m, c], load_sem.at[m, c])

    for m, c in send_order:
        load(m, c).start()
    me = dp * n_cell + cell
    load_perm = pltpu.make_async_copy(
        perm_ref.at[pl.ds(pl.multiple_of(me * width, width), width)], perm, small_sem.at[0]
    )
    load_var = pltpu.make_async_copy(var_ref, flat_table, small_sem.at[1])
    load_perm.start()
    load_var.start()

    def transfer(chunk, m, c):
        return pltpu.make_async_remote_copy(
            src_ref=outgoing.at[chunk, m, c],
            dst_ref=rows.at[chunk, me],
            send_sem=send_sem.at[chunk, m, c],
            recv_sem=recv_sem.at[chunk, m, c],
            device_id=(flip(dp, m), flip(cell, c)),
            device_id_type=MESH,
        )

    def arrival(chunk, m, c):
        return pltpu.make_async_remote_copy(
            src_ref=outgoing.at[chunk, m, c],
            dst_ref=rows.at[chunk, flip(dp, m) * n_cell + flip(cell, c)],
            send_sem=send_sem.at[chunk, m, c],
            recv_sem=recv_sem.at[chunk, m, c],
            device_id=(flip(dp, m), flip(cell, c)),
            device_id_type=MESH,
        )

    diagonal = lax.broadcasted_iota(jnp.int32, (n_rows, n_rows), 0) == lax.broadcasted_iota(
        jnp.int32, (n_rows, n_rows), 1
    )

    def look_up(index_ref, err_ref):
        n_err = err_ref.shape[0]
        index = index_ref[...].reshape(1, n_rows).astype(jnp.float32)
        index = jnp.sum(jnp.where(diagonal, index, 0.0), axis=1, keepdims=True).astype(jnp.int32)
        hit = lax.broadcasted_iota(jnp.int32, (n_rows, n_err), 1) == index
        return jnp.sum(jnp.where(hit, err_ref[...].reshape(1, n_err), 0.0), axis=1, keepdims=True)

    period_scale, site_scale = look_up(period_ref, period_err_ref), look_up(site_ref, site_err_ref)
    weight = 1.0 / jnp.sqrt(period_scale * period_scale + site_scale * site_scale)
    for chunk in range(CHUNKS):
        for place, (m, c) in enumerate(send_order):
            if chunk == 0:
                load(m, c).wait()
            at = pl.ds(chunk * chunk_width, chunk_width)
            block = (weight * stage[m, c, :, at]).astype(jnp.bfloat16)
            if m or c:
                outgoing[chunk, m, c] = block
            else:
                rows[chunk, me] = block
            if chunk == 0 and place == 0:
                pl.semaphore_wait(barrier, n_dp * n_cell - 1)
            if m or c:
                transfer(chunk, m, c).start()

    load_perm.wait()
    load_var.wait()
    t_rows, t_cols = table.shape

    @pl.loop(0, t_rows)
    def _(i):
        at = pl.ds(pl.multiple_of(i * t_cols, t_cols), t_cols)
        table[pl.ds(i, 1), :] = flat_table[at].reshape(1, t_cols)

    values = table[...]
    high = values.astype(jnp.bfloat16)
    left = values - high.astype(jnp.float32)
    middle = left.astype(jnp.bfloat16)
    low = (left - middle.astype(jnp.float32)).astype(jnp.bfloat16)
    tile = chunk_width

    @pl.loop(0, width // tile)
    def _(i):
        at = pl.ds(pl.multiple_of(i * tile, tile), tile)
        where = perm[at].reshape(1, tile)
        hit = (lax.broadcasted_iota(jnp.int32, (t_cols, tile), 0) == where % t_cols)
        hit = jnp.where(hit, 1.0, 0.0).astype(jnp.bfloat16)
        found = jnp.dot(high, hit, preferred_element_type=jnp.float32)
        found = found + jnp.dot(middle, hit, preferred_element_type=jnp.float32)
        found = found + jnp.dot(low, hit, preferred_element_type=jnp.float32)
        mine = lax.broadcasted_iota(jnp.int32, (t_rows, tile), 0) == where // t_cols
        column_var[i] = jnp.sum(jnp.where(mine, found, 0.0), axis=0, keepdims=True)

    for chunk in range(CHUNKS):
        for m, c in send_order:
            if m or c:
                arrival(chunk, m, c).wait_recv()

        @pl.loop(0, n_dp)
        def _(group):
            first = group * n_cell

            @pl.loop(0, n_cell)
            def _(c):
                block = rows[chunk, first + c].astype(jnp.float32) * column_var[chunk]
                weighted[first + c] = block.astype(jnp.bfloat16)

            right_rows = weighted[pl.ds(first, n_cell)].reshape(plane, chunk_width)
            left_rows = rows[chunk].reshape(n_total, chunk_width)
            cols = pl.ds(pl.multiple_of(group * plane, plane), plane)
            term = against(left_rows, right_rows)
            if chunk == 0:
                partial[:, cols] = term
            else:
                partial[:, cols] += term

    part, out_cols = n_total // n_cell, n_total // n_dp
    piece_rows = part // PIECES
    numbers, count = [], 0
    for steps in rounds:
        numbers.append(list(range(count, count + len(steps))))
        count += len(steps)

    def rows_of(block, piece):
        return pl.ds(pl.multiple_of(block * part + piece * piece_rows, piece_rows), piece_rows)

    def columns_of(index):
        return pl.ds(pl.multiple_of(index * out_cols, out_cols), out_cols)

    def exchanges(number, piece):
        axis, bit, left_bits, half, kind = flat[number]
        found = []
        for slot, sub in enumerate(subsets(left_bits)):
            if axis == "cell":
                n_cols = n_total if half is None else n_total // 2
                cols = pl.ds(0 if half is None else half * n_cols, n_cols)
                there = (rows_of(flip(cell, (1 << bit) ^ sub), piece), cols)
                here = (rows_of(flip(cell, sub), piece), cols)
                device = (dp, flip(cell, 1 << bit))
            else:
                mine = rows_of(cell, piece)
                there = (mine, columns_of(flip(dp, (1 << bit) ^ sub)))
                here = (mine, columns_of(flip(dp, sub)))
                device = (flip(dp, 1 << bit), cell)
            source = partial.at[there] if kind == jnp.float32 else leaving[number].at[piece, slot]
            copy = pltpu.make_async_remote_copy(
                src_ref=source,
                dst_ref=arrived[number].at[piece, slot],
                send_sem=sum_send.at[number, piece, slot],
                recv_sem=sum_recv.at[number, piece, slot],
                device_id=device,
                device_id_type=MESH,
            )
            found.append((copy, slot, there, here))
        return found

    def begin(steps, piece):
        for number in steps:
            for copy, slot, there, _ in exchanges(number, piece):
                if leaving[number] is not None:
                    leaving[number][piece, slot] = partial[there].astype(leaving[number].dtype)
                copy.start()

    def finish(steps, piece):
        for number in steps:
            for copy, slot, _, here in exchanges(number, piece):
                copy.wait_recv()
                partial[here] += arrived[number][piece, slot].astype(jnp.float32)

    for depth, steps in enumerate(numbers):
        for piece in range(PIECES):
            if depth:
                finish(numbers[depth - 1], piece)
            begin(steps, piece)
    for piece in range(PIECES):
        finish(numbers[-1], piece)
        out_ref[pl.ds(piece * piece_rows, piece_rows)] = partial[rows_of(cell, piece), columns_of(dp)]

    for number in range(count):
        for piece in range(PIECES):
            for copy, *_ in exchanges(number, piece):
                copy.wait_send()
    for chunk in range(CHUNKS):
        for m, c in send_order:
            if m or c:
                transfer(chunk, m, c).wait_send()


def body_vmem(sensitivity, row_period, row_site, period_err, site_err, cell_var, cell_perm):
    n_dp, n_cell = lax.axis_size("dp"), lax.axis_size("cell")
    n_rows, n_all = sensitivity.shape
    width = n_all // (n_dp * n_cell)
    n_total = n_rows * n_dp * n_cell
    part = n_total // n_cell
    t_cols = min(512, n_all)
    flat = [step for steps in halvings(n_dp, n_cell) for step in steps]
    bufs = [pltpu.VMEM(step_shape(step, n_dp, n_cell, n_total), step[-1]) for step in flat]
    bufs += [
        pltpu.VMEM(step_shape(step, n_dp, n_cell, n_total), step[-1]) for step in flat if step[-1] != jnp.float32
    ]
    sums = (len(flat), PIECES, n_cell // 2 + n_dp // 2)
    hbm, vmem = pl.BlockSpec(memory_space=pl.ANY), pl.BlockSpec(memory_space=pltpu.VMEM)
    chunk_width = width // CHUNKS
    return pl.pallas_call(
        functools.partial(gram_kernel, n_dp, n_cell),
        out_shape=jax.ShapeDtypeStruct((part, n_total // n_dp), jnp.float32),
        in_specs=[hbm, vmem, vmem, vmem, vmem, hbm, hbm],
        out_specs=vmem,
        scratch_shapes=[
            pltpu.VMEM((n_dp, n_cell, n_rows, width), jnp.float32),
            pltpu.VMEM((CHUNKS, n_dp, n_cell, n_rows, chunk_width), jnp.bfloat16),
            pltpu.VMEM((CHUNKS, n_dp * n_cell, n_rows, chunk_width), jnp.bfloat16),
            pltpu.VMEM((n_dp * n_cell, n_rows, chunk_width), jnp.bfloat16),
            pltpu.VMEM((width,), jnp.int32),
            pltpu.VMEM((n_all,), jnp.float32),
            pltpu.VMEM((n_all // t_cols, t_cols), jnp.float32),
            pltpu.VMEM((CHUNKS, 1, chunk_width), jnp.float32),
            pltpu.VMEM((n_total, n_total), jnp.float32),
            *bufs,
            pltpu.SemaphoreType.DMA((n_dp, n_cell)),
            pltpu.SemaphoreType.DMA((2,)),
            pltpu.SemaphoreType.DMA((CHUNKS, n_dp, n_cell)),
            pltpu.SemaphoreType.DMA((CHUNKS, n_dp, n_cell)),
            pltpu.SemaphoreType.DMA(sums),
            pltpu.SemaphoreType.DMA(sums),
        ],
        compiler_params=pltpu.CompilerParams(
            collective_id=0, has_side_effects=True, vmem_limit_bytes=VMEM_BUDGET
        ),
        cost_estimate=pl.CostEstimate(
            flops=2 * n_total * n_total * width, bytes_accessed=4 * n_rows * n_all, transcendentals=0
        ),
    )(sensitivity, row_period, row_site, period_err, site_err, cell_perm, cell_var)


def is_power_of_two(n):
    return n & (n - 1) == 0


def body(*arrays):
    sensitivity = arrays[0]
    n_dp, n_cell = lax.axis_size("dp"), lax.axis_size("cell")
    n_rows, n_all = sensitivity.shape
    n_total = n_rows * n_dp * n_cell
    need = (4 + 2 + 2 + 2) * n_rows * n_all + 2 * 4 * n_total * n_total
    width = n_all // (n_dp * n_cell)
    fits = n_total // n_cell % (16 * PIECES) == 0 and width % (128 * CHUNKS) == 0 and need < VMEM_BUDGET and is_power_of_two(n_dp) and is_power_of_two(n_cell) and n_cell > 1
    return (body_vmem if fits else body_general)(*arrays)


def solution(mesh):
    return jax.shard_map(
        body,
        mesh=mesh,
        in_specs=(
            P(("dp", "cell"), None),
            P(("dp", "cell")),
            P(("dp", "cell")),
            P(),
            P(),
            P(),
            P(),
        ),
        out_specs=P("cell", "dp"),
        check_vma=False,
    )
```

```python
import functools
import jax
import jax.numpy as jnp
from jax import lax
from jax.experimental import pallas as pl
from jax.experimental.pallas import tpu as pltpu
from jax.sharding import PartitionSpec as P

MESH = pl.DeviceIdType.MESH
VMEM_BUDGET = 56 * 1024 * 1024
PIECES = 2
CHUNKS = 4


def weigh_rows(row_period, row_site, period_err, site_err):
    period_hit = row_period[:, None] == jnp.arange(period_err.shape[0], dtype=jnp.int32)[None, :]
    site_hit = row_site[:, None] == jnp.arange(site_err.shape[0], dtype=jnp.int32)[None, :]
    period_scale = jnp.sum(jnp.where(period_hit, period_err[None, :], 0.0), axis=1)
    site_scale = jnp.sum(jnp.where(site_hit, site_err[None, :], 0.0), axis=1)
    return 1.0 / jnp.sqrt(period_scale * period_scale + site_scale * site_scale)


def pack_rows(sensitivity, row_period, row_site, period_err, site_err):
    row_weight = weigh_rows(row_period, row_site, period_err, site_err)
    return (row_weight[:, None] * sensitivity).astype(jnp.bfloat16)


def weigh_columns(scaled, cell_var, cell_perm, first_cell):
    width = scaled.shape[1]
    positions = lax.dynamic_slice_in_dim(cell_perm, first_cell, width)
    column_var = cell_var[positions]
    return (scaled.astype(jnp.float32) * column_var[None, :]).astype(jnp.bfloat16)


def against(rows_block, weighted):
    return lax.dot_general(
        rows_block, weighted, (((1,), (1,)), ((), ())), preferred_element_type=jnp.float32
    )


def body_general(sensitivity, row_period, row_site, period_err, site_err, cell_var, cell_perm):
    packed = pack_rows(sensitivity, row_period, row_site, period_err, site_err)
    total_cells = cell_var.shape[0]
    scaled = lax.all_to_all(packed, "cell", split_axis=1, concat_axis=0, tiled=True)
    first_cell = lax.axis_index("cell") * (total_cells // lax.axis_size("cell"))
    weighted = weigh_columns(scaled, cell_var, cell_perm, first_cell)
    partial_value = against(lax.all_gather(scaled, "dp", axis=0, tiled=True), weighted)
    gram = lax.psum_scatter(partial_value, "cell", scatter_dimension=0, tiled=True)
    return gram


def flip(index, mask):
    bit = 1
    while bit <= mask:
        if mask & bit:
            index = index + (1 - 2 * ((index // bit) % 2)) * bit
        bit *= 2
    return index


def subsets(bits):
    masks = [0]
    for bit in bits:
        masks = masks + [mask | (1 << bit) for mask in masks]
    return masks


def halvings(n_dp, n_cell):
    levels = n_cell.bit_length() - 1
    rest = list(range(1, levels))
    orders = (rest, rest[::-1])
    rounds = [[("cell", 0, rest, None, jnp.float32)]]
    for depth in range(len(rest)):
        rounds.append([
            ("cell", order[depth], order[depth + 1:], half, jnp.float32) for half, order in enumerate(orders)
        ])
    dp_levels = n_dp.bit_length() - 1
    for bit in range(dp_levels):
        rounds.append([("dp", bit, list(range(bit + 1, dp_levels)), None, jnp.float32)])
    return rounds


def step_shape(step, n_dp, n_cell, n_total):
    axis, _, left_bits, half, _ = step
    n_cols = n_total // n_dp if axis == "dp" else n_total if half is None else n_total // 2
    return (PIECES, 1 << len(left_bits), n_total // n_cell // PIECES, n_cols)


def gram_kernel(
    n_dp, n_cell,
    sens_ref, period_ref, site_ref, period_err_ref, site_err_ref, perm_ref, var_ref, out_ref,
    stage, outgoing, rows, weighted, perm, flat_table, table, column_var, partial, *rest,
):
    rounds = halvings(n_dp, n_cell)
    flat = [step for steps in rounds for step in steps]
    rest = list(rest)
    arrived = [rest.pop(0) for _ in flat]
    leaving = [rest.pop(0) if step[-1] != jnp.float32 else None for step in flat]
    load_sem, small_sem, send_sem, recv_sem, sum_send, sum_recv = rest
    dp, cell = lax.axis_index("dp"), lax.axis_index("cell")
    n_rows, n_all = sens_ref.shape
    width = n_all // (n_dp * n_cell)
    plane = n_cell * n_rows
    n_total = n_dp * plane
    chunk_width = width // CHUNKS
    far = [m for m in reversed(range(n_dp)) if m >= n_dp // 2]
    near = [m for m in reversed(range(n_dp)) if m < n_dp // 2]
    masks = [m for pair in zip(far, near) for m in pair] if near else far
    spread = [c for low in range(n_cell // 2) for c in (n_cell - 1 - low, low)]
    send_order = [(m, c if m in far else n_cell - 1 - c) for c in spread for m in masks]

    barrier = pltpu.get_barrier_semaphore()
    for m in range(n_dp):
        for c in range(n_cell):
            if m or c:
                pl.semaphore_signal(barrier, inc=1, device_id=(flip(dp, m), flip(cell, c)), device_id_type=MESH)

    def load(m, c):
        first = pl.multiple_of((flip(dp, m) * n_cell + flip(cell, c)) * width, 128)
        return pltpu.make_async_copy(sens_ref.at[:, pl.ds(first, width)], stage.at[m, c], load_sem.at[m, c])

    for m, c in send_order:
        load(m, c).start()
    me = dp * n_cell + cell
    load_perm = pltpu.make_async_copy(
        perm_ref.at[pl.ds(pl.multiple_of(me * width, width), width)], perm, small_sem.at[0]
    )
    load_var = pltpu.make_async_copy(var_ref, flat_table, small_sem.at[1])
    load_perm.start()
    load_var.start()

    def transfer(chunk, m, c):
        return pltpu.make_async_remote_copy(
            src_ref=outgoing.at[chunk, m, c],
            dst_ref=rows.at[chunk, me],
            send_sem=send_sem.at[chunk, m, c],
            recv_sem=recv_sem.at[chunk, m, c],
            device_id=(flip(dp, m), flip(cell, c)),
            device_id_type=MESH,
        )

    def arrival(chunk, m, c):
        return pltpu.make_async_remote_copy(
            src_ref=outgoing.at[chunk, m, c],
            dst_ref=rows.at[chunk, flip(dp, m) * n_cell + flip(cell, c)],
            send_sem=send_sem.at[chunk, m, c],
            recv_sem=recv_sem.at[chunk, m, c],
            device_id=(flip(dp, m), flip(cell, c)),
            device_id_type=MESH,
        )

    diagonal = lax.broadcasted_iota(jnp.int32, (n_rows, n_rows), 0) == lax.broadcasted_iota(
        jnp.int32, (n_rows, n_rows), 1
    )

    def look_up(index_ref, err_ref):
        n_err = err_ref.shape[0]
        index = index_ref[...].reshape(1, n_rows).astype(jnp.float32)
        index = jnp.sum(jnp.where(diagonal, index, 0.0), axis=1, keepdims=True).astype(jnp.int32)
        hit = lax.broadcasted_iota(jnp.int32, (n_rows, n_err), 1) == index
        return jnp.sum(jnp.where(hit, err_ref[...].reshape(1, n_err), 0.0), axis=1, keepdims=True)

    period_scale, site_scale = look_up(period_ref, period_err_ref), look_up(site_ref, site_err_ref)
    weight = 1.0 / jnp.sqrt(period_scale * period_scale + site_scale * site_scale)
    for chunk in range(CHUNKS):
        for place, (m, c) in enumerate(send_order):
            if chunk == 0:
                load(m, c).wait()
            at = pl.ds(chunk * chunk_width, chunk_width)
            block = (weight * stage[m, c, :, at]).astype(jnp.bfloat16)
            if m or c:
                outgoing[chunk, m, c] = block
            else:
                rows[chunk, me] = block
            if chunk == 0 and place == 0:
                pl.semaphore_wait(barrier, n_dp * n_cell - 1)
            if m or c:
                transfer(chunk, m, c).start()

    load_perm.wait()
    load_var.wait()
    t_rows, t_cols = table.shape

    @pl.loop(0, t_rows)
    def _(i):
        at = pl.ds(pl.multiple_of(i * t_cols, t_cols), t_cols)
        table[pl.ds(i, 1), :] = flat_table[at].reshape(1, t_cols)

    values = table[...]
    high = values.astype(jnp.bfloat16)
    left = values - high.astype(jnp.float32)
    middle = left.astype(jnp.bfloat16)
    low = (left - middle.astype(jnp.float32)).astype(jnp.bfloat16)
    tile = chunk_width

    @pl.loop(0, width // tile)
    def _(i):
        at = pl.ds(pl.multiple_of(i * tile, tile), tile)
        where = perm[at].reshape(1, tile)
        hit = (lax.broadcasted_iota(jnp.int32, (t_cols, tile), 0) == where % t_cols)
        hit = jnp.where(hit, 1.0, 0.0).astype(jnp.bfloat16)
        found = jnp.dot(high, hit, preferred_element_type=jnp.float32)
        found = found + jnp.dot(middle, hit, preferred_element_type=jnp.float32)
        found = found + jnp.dot(low, hit, preferred_element_type=jnp.float32)
        mine = lax.broadcasted_iota(jnp.int32, (t_rows, tile), 0) == where // t_cols
        column_var[i] = jnp.sum(jnp.where(mine, found, 0.0), axis=0, keepdims=True)

    for chunk in range(CHUNKS):
        for m, c in send_order:
            if m or c:
                arrival(chunk, m, c).wait_recv()

        @pl.loop(0, n_dp)
        def _(group):
            first = group * n_cell

            @pl.loop(0, n_cell)
            def _(c):
                block = rows[chunk, first + c].astype(jnp.float32) * column_var[chunk]
                weighted[first + c] = block.astype(jnp.bfloat16)

            right_rows = weighted[pl.ds(first, n_cell)].reshape(plane, chunk_width)
            left_rows = rows[chunk].reshape(n_total, chunk_width)
            cols = pl.ds(pl.multiple_of(group * plane, plane), plane)
            term = against(left_rows, right_rows)
            if chunk == 0:
                partial[:, cols] = term
            else:
                partial[:, cols] += term

    part, out_cols = n_total // n_cell, n_total // n_dp
    piece_rows = part // PIECES
    numbers, count = [], 0
    for steps in rounds:
        numbers.append(list(range(count, count + len(steps))))
        count += len(steps)

    def rows_of(block, piece):
        return pl.ds(pl.multiple_of(block * part + piece * piece_rows, piece_rows), piece_rows)

    def columns_of(index):
        return pl.ds(pl.multiple_of(index * out_cols, out_cols), out_cols)

    def exchanges(number, piece):
        axis, bit, left_bits, half, kind = flat[number]
        found = []
        for slot, sub in enumerate(subsets(left_bits)):
            if axis == "cell":
                n_cols = n_total if half is None else n_total // 2
                cols = pl.ds(0 if half is None else half * n_cols, n_cols)
                there = (rows_of(flip(cell, (1 << bit) ^ sub), piece), cols)
                here = (rows_of(flip(cell, sub), piece), cols)
                device = (dp, flip(cell, 1 << bit))
            else:
                mine = rows_of(cell, piece)
                there = (mine, columns_of(flip(dp, (1 << bit) ^ sub)))
                here = (mine, columns_of(flip(dp, sub)))
                device = (flip(dp, 1 << bit), cell)
            source = partial.at[there] if kind == jnp.float32 else leaving[number].at[piece, slot]
            copy = pltpu.make_async_remote_copy(
                src_ref=source,
                dst_ref=arrived[number].at[piece, slot],
                send_sem=sum_send.at[number, piece, slot],
                recv_sem=sum_recv.at[number, piece, slot],
                device_id=device,
                device_id_type=MESH,
            )
            found.append((copy, slot, there, here))
        return found

    def begin(steps, piece):
        for number in steps:
            for copy, slot, there, _ in exchanges(number, piece):
                if leaving[number] is not None:
                    leaving[number][piece, slot] = partial[there].astype(leaving[number].dtype)
                copy.start()

    def finish(steps, piece):
        for number in steps:
            for copy, slot, _, here in exchanges(number, piece):
                copy.wait_recv()
                partial[here] += arrived[number][piece, slot].astype(jnp.float32)

    for depth, steps in enumerate(numbers):
        for piece in range(PIECES):
            if depth:
                finish(numbers[depth - 1], piece)
            begin(steps, piece)
    for piece in range(PIECES):
        finish(numbers[-1], piece)
        out_ref[pl.ds(piece * piece_rows, piece_rows)] = partial[rows_of(cell, piece), columns_of(dp)]

    for number in range(count):
        for piece in range(PIECES):
            for copy, *_ in exchanges(number, piece):
                copy.wait_send()
    for chunk in range(CHUNKS):
        for m, c in send_order:
            if m or c:
                transfer(chunk, m, c).wait_send()


def body_vmem(sensitivity, row_period, row_site, period_err, site_err, cell_var, cell_perm):
    n_dp, n_cell = lax.axis_size("dp"), lax.axis_size("cell")
    n_rows, n_all = sensitivity.shape
    width = n_all // (n_dp * n_cell)
    n_total = n_rows * n_dp * n_cell
    part = n_total // n_cell
    t_cols = min(512, n_all)
    flat = [step for steps in halvings(n_dp, n_cell) for step in steps]
    bufs = [pltpu.VMEM(step_shape(step, n_dp, n_cell, n_total), step[-1]) for step in flat]
    bufs += [
        pltpu.VMEM(step_shape(step, n_dp, n_cell, n_total), step[-1]) for step in flat if step[-1] != jnp.float32
    ]
    sums = (len(flat), PIECES, n_cell // 2 + n_dp // 2)
    hbm, vmem = pl.BlockSpec(memory_space=pl.ANY), pl.BlockSpec(memory_space=pltpu.VMEM)
    chunk_width = width // CHUNKS
    return pl.pallas_call(
        functools.partial(gram_kernel, n_dp, n_cell),
        out_shape=jax.ShapeDtypeStruct((part, n_total // n_dp), jnp.float32),
        in_specs=[hbm, vmem, vmem, vmem, vmem, hbm, hbm],
        out_specs=vmem,
        scratch_shapes=[
            pltpu.VMEM((n_dp, n_cell, n_rows, width), jnp.float32),
            pltpu.VMEM((CHUNKS, n_dp, n_cell, n_rows, chunk_width), jnp.bfloat16),
            pltpu.VMEM((CHUNKS, n_dp * n_cell, n_rows, chunk_width), jnp.bfloat16),
            pltpu.VMEM((n_dp * n_cell, n_rows, chunk_width), jnp.bfloat16),
            pltpu.VMEM((width,), jnp.int32),
            pltpu.VMEM((n_all,), jnp.float32),
            pltpu.VMEM((n_all // t_cols, t_cols), jnp.float32),
            pltpu.VMEM((CHUNKS, 1, chunk_width), jnp.float32),
            pltpu.VMEM((n_total, n_total), jnp.float32),
            *bufs,
            pltpu.SemaphoreType.DMA((n_dp, n_cell)),
            pltpu.SemaphoreType.DMA((2,)),
            pltpu.SemaphoreType.DMA((CHUNKS, n_dp, n_cell)),
            pltpu.SemaphoreType.DMA((CHUNKS, n_dp, n_cell)),
            pltpu.SemaphoreType.DMA(sums),
            pltpu.SemaphoreType.DMA(sums),
        ],
        compiler_params=pltpu.CompilerParams(
            collective_id=0, has_side_effects=True, vmem_limit_bytes=VMEM_BUDGET
        ),
        cost_estimate=pl.CostEstimate(
            flops=2 * n_total * n_total * width, bytes_accessed=4 * n_rows * n_all, transcendentals=0
        ),
    )(sensitivity, row_period, row_site, period_err, site_err, cell_perm, cell_var)


def is_power_of_two(n):
    return n & (n - 1) == 0


def body(*arrays):
    sensitivity = arrays[0]
    n_dp, n_cell = lax.axis_size("dp"), lax.axis_size("cell")
    n_rows, n_all = sensitivity.shape
    n_total = n_rows * n_dp * n_cell
    need = (4 + 2 + 2 + 2) * n_rows * n_all + 2 * 4 * n_total * n_total
    width = n_all // (n_dp * n_cell)
    fits = n_total // n_cell % (16 * PIECES) == 0 and width % (128 * CHUNKS) == 0 and need < VMEM_BUDGET and is_power_of_two(n_dp) and is_power_of_two(n_cell) and n_cell > 1
    return (body_vmem if fits else body_general)(*arrays)


def solution(mesh):
    return jax.shard_map(
        body,
        mesh=mesh,
        in_specs=(
            P(("dp", "cell"), None),
            P(("dp", "cell")),
            P(("dp", "cell")),
            P(),
            P(),
            P(),
            P(),
        ),
        out_specs=P("cell", "dp"),
        check_vma=False,
    )
```
